128 devices in a mesh: row: 8 (over y, core), col: 16 (over z, x).
Axes of the slice: x: 4, y: 4, z: 4, core: 2. Of those that a mesh axis runs over, the one named last changes fastest.
Arguments:
- inputs: bfloat16 [2048, 6144], P('col', 'row'), may hold values from -1200 to 1200
- norm_gain: float32 [6144], P('row'), may hold values from 0.5 to 9
- weight_in: bfloat16 [6144, 24576], P('row', 'col'), may hold values from -1 to 1
- weight_out: bfloat16 [24576, 6144], P('col', 'row'), may hold values from -0.0390625 to 0.0390625
- cotangent: bfloat16 [2048, 6144], P('col', 'row'), may hold values from -4 to 4
Outputs:
- branch: bfloat16 [2048, 6144], P('col', 'row')
- input_gradient: bfloat16 [2048, 6144], P('col', 'row')
- in_gradient: float32 [6144, 24576], P('row', 'col')
- out_gradient: float32 [24576, 6144], P('col', 'row')
- gain_gradient: float32 [6144], P('row')
The draws below stay inside these ranges and needn't reach their ends.
All inputs are finite; a program needn't handle non-finite values.
Results may differ from the reference program's by a relative error of at most 0.039.
Values may be sent and summed in bfloat16 or wider, within the bound.
No kernel may reach another device: no remote copies, remote signals or barrier semaphores. Data moves between devices by JAX's collectives and lax.ppermute only.
A program may use at most 128 MiB of HBM per device.

```python
import jax
import jax.numpy as jnp
from jax import lax

D = 6144
FF = 24576
TOKENS = 2048
N_ROW = 8
N_COL = 16


def draw_inputs(key, part):
    key = jax.random.fold_in(key, 11)
    first, second, third = jax.random.split(key, 3)
    rising = 3.0 ** (jnp.arange(D, dtype=jnp.float32) / (D - 1))
    column_scale = rising[None, :] * 10.0 ** (0.5 * jax.random.uniform(third, (1, D), jnp.float32))
    noise = jax.random.truncated_normal(first, -6.0, 6.0, (TOKENS, D), jnp.float32)
    row_scale = 10.0 ** jax.random.uniform(second, (TOKENS, 1), jnp.float32)
    values = noise * row_scale * column_scale
    return values.astype(jnp.bfloat16)


def draw_norm_gain(key, part):
    key = jax.random.fold_in(key, 12)
    position = jnp.arange(D, dtype=jnp.float32) / (D - 1)
    factor = jax.random.uniform(key, (D,), jnp.float32, minval=0.6, maxval=1.4)
    values = factor * 3.0 ** position
    return values.astype(jnp.float32)


def draw_weight_in(key, part):
    key = jax.random.fold_in(key, 13)
    first, second = jax.random.split(key, 2)
    shared = jax.random.truncated_normal(second, -3.0, 3.0, (1, FF), jnp.float32)
    noise = jax.random.truncated_normal(first, -4.0, 4.0, (D, FF), jnp.float32)
    values = (noise + shared) * (1.0 / jnp.sqrt(jnp.float32(D)))
    return values.astype(jnp.bfloat16)


def shard_levels(key, shape, cuts, low, high):
    loudness, own = 1.0, jax.random.fold_in(key, 6)
    for dim, blocks in cuts:
        steps = jnp.exp(jax.random.uniform(jax.random.fold_in(own, dim), (blocks,), jnp.float32, low / len(cuts), high / len(cuts)))
        loudness = loudness * jnp.repeat(steps, shape[dim] // blocks).reshape([-1 if axis == dim else 1 for axis in range(len(shape))])
    return loudness


def gaussian(stream_key, shape, scale, limit, cuts=(), kind=jnp.bfloat16):
    loudness = shard_levels(stream_key, shape, cuts, -0.22, 0.18) if cuts else 1.0
    entries = jax.random.normal(stream_key, shape, jnp.float32) * scale * loudness
    return jnp.minimum(jnp.maximum(entries, -limit), limit).astype(kind)


def setup_inputs(seed: int = 0) -> dict:
    keys = jax.random.split(jax.random.key(seed), 6)
    return {
        "inputs": draw_inputs(jax.random.fold_in(keys[5], 71), 0),
        "norm_gain": draw_norm_gain(jax.random.fold_in(keys[5], 71), 0),
        "weight_in": draw_weight_in(jax.random.fold_in(keys[5], 71), 0),
        "weight_out": gaussian(keys[3], (FF, D), FF ** -0.5, 0.0390625, ((0, 16), (1, 8))),
        "cotangent": gaussian(keys[4], (TOKENS, D), 0.25, 4.0, ((0, 16), (1, 8))),
    }


epsilon = 1e-06

def gelu_value(value):
    return jax.nn.gelu(value, approximate=False)

def gelu_slope(value, upstream):
    return jax.vjp(gelu_value, value)[1](upstream)[0]

def rounded(term):
    return lax.optimization_barrier(term.astype(jnp.bfloat16)).astype(jnp.float32)

def block_sum(left, right, blocks, right_rows):
    width = left.shape[1] // blocks
    out_cols = right.shape[1] if right_rows else right.shape[0]

    def advance(block, total):
        start = (block * width).astype(jnp.int32)
        piece = lax.dynamic_slice_in_dim(left, start, width, 1)
        if right_rows:
            other = lax.dynamic_slice_in_dim(right, start, width, 0)
            term = jnp.dot(piece, other, preferred_element_type=jnp.float32)
        else:
            other = lax.dynamic_slice_in_dim(right, start, width, 1)
            term = lax.dot_general(piece, other, (((1,), (1,)), ((), ())), preferred_element_type=jnp.float32)
        return total + rounded(term)
    return lax.fori_loop(0, blocks, advance, jnp.zeros((left.shape[0], out_cols), jnp.float32))

def reference(inputs, norm_gain, weight_in, weight_out, cotangent):
    floats = inputs.astype(jnp.float32)
    center = lax.optimization_barrier(jnp.sum(floats, axis=1)) / D
    meansq = lax.optimization_barrier(jnp.sum(floats * floats, axis=1)) / D
    spread = lax.rsqrt(meansq - center * center + epsilon)
    normed = (floats - center[:, None]) * spread[:, None]
    scaled = (normed * norm_gain[None, :]).astype(jnp.bfloat16)
    hidden = block_sum(scaled, weight_in, N_ROW, True)
    active = gelu_value(hidden).astype(jnp.bfloat16)
    branch = block_sum(active, weight_out, N_COL, True).astype(jnp.bfloat16)
    active_gradient = block_sum(cotangent, weight_out, N_ROW, False)
    hidden_gradient = gelu_slope(hidden, active_gradient).astype(jnp.bfloat16)
    out_gradient = lax.dot_general(active, cotangent, (((0,), (0,)), ((), ())), preferred_element_type=jnp.float32)
    in_gradient = lax.dot_general(scaled, hidden_gradient, (((0,), (0,)), ((), ())), preferred_element_type=jnp.float32)
    normed_gradient = block_sum(hidden_gradient, weight_in, N_COL, False)
    gain_gradient = lax.optimization_barrier(jnp.sum(normed_gradient * normed, axis=0))
    scaled_gradient = normed_gradient * norm_gain[None, :]
    mean_gradient = lax.optimization_barrier(jnp.sum(scaled_gradient, axis=1)) / D
    mean_cross = lax.optimization_barrier(jnp.sum(scaled_gradient * normed, axis=1)) / D
    input_gradient = spread[:, None] * (scaled_gradient - mean_gradient[:, None] - normed * mean_cross[:, None])
    return (branch, input_gradient.astype(jnp.bfloat16), in_gradient, out_gradient, gain_gradient)
```

```python
import jax
import jax.numpy as jnp
from jax import lax
from jax.sharding import PartitionSpec as P

D = 6144
SIDE = 4
SLOT_ORDER = (0, 3, 2, 1)
epsilon = 1e-06
SQRT_HALF = 0.7071067811865476
PDF_SCALE = 0.3989422804014327


def device(x, y, z, core):
    return ((y % SIDE) * 2 + core) * SIDE * SIDE + (z % SIDE) * SIDE + x % SIDE


def table(target):
    pairs = []
    for x in range(SIDE):
        for y in range(SIDE):
            for z in range(SIDE):
                for core in range(2):
                    pairs.append((device(x, y, z, core), device(*target(x, y, z, core))))
    return pairs


def send(value, target):
    return lax.ppermute(value, ("row", "col"), table(target))


def to_sibling(value):
    return send(value, lambda x, y, z, core: (x, y, z, 1 - core))


def to_ring(value):
    return send(value, lambda x, y, z, core: (x, y + 1 - 2 * core, z, core))


def to_first(value, step):
    return send(
        value,
        lambda x, y, z, core: (x + step, y, z, core) if core == 0 else (x, y, z + step, core),
    )


def to_second(value, slot, sign):
    def target(x, y, z, core):
        step = sign * ((y + (1 - 2 * core) * slot) % SIDE)
        return (x, y, z + step, core) if core == 0 else (x + step, y, z, core)

    return send(value, target)


def after(value, *done):
    return lax.optimization_barrier((value, *done))[0]


def gather_line(own):
    return jnp.concatenate([own] + [to_first(own, -step) for step in (1, 2, 3)], axis=0)


def gather_slots(line):
    three, two = to_second(line, 3, -1), to_second(line, 2, -1)
    line = after(line, three)
    one, zero = to_second(line, 1, -1), to_second(line, 0, -1)
    return [zero, one, two, three]


def scatter_slots(parts, product):
    got = []
    for slot in SLOT_ORDER:
        part = after(parts[slot], got[-2]) if len(got) >= 2 else parts[slot]
        last = product(part).astype(jnp.bfloat16)
        got.append(to_second(last, slot, 1))
    return got, last


def scatter_line(got):
    line = sum(piece.astype(jnp.float32) for piece in got)
    rows = line.shape[0] // SIDE
    total = line[:rows]
    low = line.astype(jnp.bfloat16)
    for step in (1, 2, 3):
        total = total + to_first(low[step * rows : (step + 1) * rows], step).astype(jnp.float32)
    return total


def scatter_y(parts, product):
    running = product(parts[3])
    for slot in (2, 1, 0):
        running = product(parts[slot]) + to_ring(running.astype(jnp.bfloat16)).astype(jnp.float32)
    return running


def dot(left, right):
    return jnp.dot(left, right, preferred_element_type=jnp.float32)


def dot_rows(left, right):
    return lax.dot_general(left, right, (((1,), (1,)), ((), ())), preferred_element_type=jnp.float32)


def dot_tokens(left, right):
    return lax.dot_general(left, right, (((0,), (0,)), ((), ())), preferred_element_type=jnp.float32)


def sum_y(value):
    value = value + send(value, lambda x, y, z, core: (x, y ^ 1, z, core))
    return value + send(value, lambda x, y, z, core: (x, y ^ 2, z, core))


def sum_col(value):
    value = value + send(value, lambda x, y, z, core: (x ^ 1, y, z, core))
    value = value + send(value, lambda x, y, z, core: (x, y, z ^ 1, core))
    value = value + send(value, lambda x, y, z, core: (x ^ 2, y, z, core))
    return value + send(value, lambda x, y, z, core: (x, y, z ^ 2, core))


def my_half(value, core):
    halves = value.reshape(2, value.shape[0] // 2, value.shape[1])
    mine = lax.dynamic_index_in_dim(halves, core, 0, keepdims=False)
    other = lax.dynamic_index_in_dim(halves, 1 - core, 0, keepdims=False)
    return mine, other


def both_halves(value, core):
    width = value.shape[1] // 2
    mine = value[:, :width]
    other = to_sibling(value[:, width:])
    return jnp.where(
        core == 0,
        jnp.concatenate([mine, other], axis=0),
        jnp.concatenate([other, mine], axis=0),
    )


def per_device(inputs, norm_gain, weight_in, weight_out, cotangent):
    core = lax.axis_index("row") % 2
    width = weight_in.shape[0]

    mine, other = my_half(jnp.concatenate([inputs, cotangent], axis=1), core)
    theirs = to_sibling(other)
    line = gather_line(jnp.concatenate([mine, theirs], axis=1))
    cot_line = jnp.concatenate([line[:, width : 2 * width], line[:, 3 * width :]], axis=1)
    cot = gather_slots(cot_line)
    out_weight = jnp.concatenate([weight_out, to_sibling(weight_out)], axis=1)

    gain = jnp.concatenate([norm_gain, to_sibling(norm_gain)])
    floats = jnp.concatenate([line[:, :width], line[:, 2 * width : 3 * width]], axis=1)
    floats = floats.astype(jnp.float32)
    sums = sum_y(jnp.stack([jnp.sum(floats, axis=1), jnp.sum(floats * floats, axis=1)]))
    center = sums[0] / D
    spread = lax.rsqrt(sums[1] / D - center * center + epsilon)
    normed = (floats - center[:, None]) * spread[:, None]
    scaled_line = (normed * gain[None, :]).astype(jnp.bfloat16)
    scaled = gather_slots(after(scaled_line, cot[2], cot[1]))
    in_weight = jnp.concatenate([weight_in, to_sibling(weight_in)], axis=0)
    rows = inputs.shape[0] // 2
    normed, spread = normed[:rows], spread[:rows]

    active_gradient = scatter_y(cot, lambda part: dot_rows(part, out_weight))
    hidden = scatter_y(scaled, lambda part: dot(part, in_weight))

    lower = 0.5 + 0.5 * lax.erf(hidden * SQRT_HALF)
    active = (hidden * lower).astype(jnp.bfloat16)
    slope = lower + hidden * (PDF_SCALE * jnp.exp(-0.5 * hidden * hidden))
    hidden_gradient = (active_gradient * slope).astype(jnp.bfloat16)

    gradient_three = to_ring(hidden_gradient)
    active_three = to_ring(after(active, gradient_three))
    gradient_two = to_ring(gradient_three)
    gradient_one = to_ring(gradient_two)
    active_two = to_ring(active_three)
    active_one = to_ring(active_two)
    hidden_gradients = [hidden_gradient, gradient_one, gradient_two, gradient_three]
    actives = [active, active_one, active_two, active_three]

    normed_got, _ = scatter_slots(hidden_gradients, lambda part: dot_rows(part, in_weight))
    branch_got, branch_last = scatter_slots(actives, lambda part: dot(part, out_weight))

    scaled_all = jnp.concatenate(scaled, axis=0)
    slope_all = jnp.concatenate(hidden_gradients, axis=0)
    other = to_sibling(dot_tokens(scaled_all[:, width:], slope_all).astype(jnp.bfloat16))
    in_gradient = dot_tokens(scaled_all[:, :width], slope_all) + other.astype(jnp.float32)

    normed_got[0] = after(normed_got[0], branch_last)
    normed_gradient = scatter_line(normed_got)
    gain_part = jnp.sum(normed_gradient * normed, axis=0)
    gain_gradient = sum_col(gain_part[:width] + to_sibling(gain_part[width:]))
    scaled_gradient = normed_gradient * gain[None, :]
    sums = sum_y(
        jnp.stack([jnp.sum(scaled_gradient, axis=1), jnp.sum(scaled_gradient * normed, axis=1)])
    )
    input_gradient = spread[:, None] * (
        scaled_gradient - sums[0][:, None] / D - normed * (sums[1][:, None] / D)
    )
    input_gradient = both_halves(input_gradient.astype(jnp.bfloat16), core)

    cot_all = jnp.concatenate(cot, axis=0)
    active_all = jnp.concatenate(actives, axis=0)
    other = dot_tokens(active_all, cot_all[:, width:]).astype(jnp.bfloat16)
    branch_got[0] = after(branch_got[0], in_gradient, other)
    branch = scatter_line(branch_got)
    out_gradient = dot_tokens(active_all, cot_all[:, :width]) + to_sibling(other).astype(jnp.float32)
    branch = after(branch, out_gradient)

    branch = both_halves(branch.astype(jnp.bfloat16), core)
    return (branch, input_gradient, in_gradient, out_gradient, gain_gradient)


def solution(mesh):
    in_specs = (P("col", "row"), P("row"), P("row", "col"), P("col", "row"), P("col", "row"))
    out_specs = (P("col", "row"), P("col", "row"), P("row", "col"), P("col", "row"), P("row"))
    return jax.shard_map(
        per_device, mesh=mesh, in_specs=in_specs, out_specs=out_specs, check_vma=False
    )
```

```python
import jax
import jax.numpy as jnp
from jax import lax
from jax.sharding import PartitionSpec as P

D = 6144
SIDE = 4
epsilon = 1e-06
SQRT_HALF = 0.7071067811865476
PDF_SCALE = 0.3989422804014327


def device(x, y, z, core):
    return ((y % SIDE) * 2 + core) * SIDE * SIDE + (z % SIDE) * SIDE + x % SIDE


def table(target):
    pairs = []
    for x in range(SIDE):
        for y in range(SIDE):
            for z in range(SIDE):
                for core in range(2):
                    end = target(x, y, z, core)
                    if end is not None:
                        pairs.append((device(x, y, z, core), device(*end)))
    return pairs


def send(value, target):
    return lax.ppermute(value, ("row", "col"), table(target))


def to_sibling(value):
    return send(value, lambda x, y, z, core: (x, y, z, 1 - core))


def to_ring(value):
    return send(value, lambda x, y, z, core: (x, y + 1 - 2 * core, z, core))


def to_first(value, step):
    return send(
        value,
        lambda x, y, z, core: (x + step, y, z, core) if core == 0 else (x, y, z + step, core),
    )


def second_other(value, step):
    return send(
        value,
        lambda x, y, z, core: (x, y, z + step, core) if core == 0 else (x + step, y, z, core),
    )


def second_piece(value, slot):
    def target(x, y, z, core):
        step = (y + slot) % SIDE
        if step == 0:
            return None
        return (x, y, z + step, core) if core == 0 else (x + step, y, z, core)

    return send(value, target)


def to_ring_back(value):
    return send(value, lambda x, y, z, core: (x, y - 1 + 2 * core, z, core))


def fence(*values):
    return lax.optimization_barrier(values)


def after(value, *done):
    return fence(value, *done)[0]


def low(value):
    return value.astype(jnp.bfloat16)


def wide(value):
    return value.astype(jnp.float32)


def product(left, right, by_rows, more=None, kind=jnp.bfloat16):
    contract = (((1,), (1 if by_rows else 0,)), ((), ()))
    value = lax.dot_general(left, right, contract, preferred_element_type=jnp.float32)
    if more is not None:
        value = value + wide(more)
    return value.astype(kind)


def dot_tokens(left, right):
    return lax.dot_general(left, right, (((0,), (0,)), ((), ())), preferred_element_type=jnp.float32)


def my_half(value, core):
    halves = value.reshape(2, value.shape[0] // 2, value.shape[1])
    mine = lax.dynamic_index_in_dim(halves, core, 0, keepdims=False)
    other = lax.dynamic_index_in_dim(halves, 1 - core, 0, keepdims=False)
    return mine, other


def y_other(value, step):
    return send(value, lambda x, y, z, core: (x, y + step, z, core))


def gather_line(own):
    return jnp.concatenate([own] + [to_first(own, -step) for step in (1, 2, 3)], axis=0)


def by_slot(blocks, y):
    rows, columns = blocks[0].shape
    buffer = jnp.zeros((SIDE * rows, columns), blocks[0].dtype)
    for step, block in enumerate(blocks):
        slot = (step - y) % SIDE
        buffer = lax.dynamic_update_slice(buffer, block, (slot * rows, 0))
    return buffer


def per_device(inputs, norm_gain, weight_in, weight_out, cotangent):
    row = lax.axis_index("row")
    core, y = row % 2, row // 2
    lower_core = core == 0
    home = (SIDE - y) % SIDE
    width = weight_in.shape[0]
    rows = inputs.shape[0] // 2

    mine, other = my_half(jnp.concatenate([inputs, cotangent], axis=1), core)
    theirs = to_sibling(other)
    their_out = to_sibling(weight_out)
    their_gain = to_sibling(norm_gain)
    floats = wide(jnp.concatenate([mine[:, :width], theirs[:, :width]], axis=1))
    own_cot = jnp.concatenate([mine[:, width:], theirs[:, width:]], axis=1)

    sums = jnp.stack([jnp.sum(floats, axis=1), jnp.sum(floats * floats, axis=1)])
    cot_line = gather_line(own_cot)
    sums = sums + send(sums, lambda x, y, z, core: (x, y ^ 1, z, core))
    cot_line, sums, their_gain = fence(cot_line, sums, their_gain)

    cot_blocks = [cot_line] + [second_other(cot_line, -step) for step in (1, 2, 3)]
    swapped = send(sums, lambda x, y, z, core: (x, y ^ 2, z, core))
    out_weight = jnp.concatenate([weight_out, their_out], axis=1)
    *cot_blocks, sums, swapped, out_weight, floats = fence(
        *cot_blocks, sums, swapped, out_weight, floats
    )

    cot_all = by_slot(cot_blocks, y)
    line_rows = cot_line.shape[0]
    cots = [cot_all[slot * line_rows : (slot + 1) * line_rows] for slot in range(SIDE)]
    got = to_ring(product(cots[2], out_weight, True))
    sums = sums + swapped
    center = sums[0] / D
    spread = lax.rsqrt(sums[1] / D - center * center + epsilon)
    normed = (floats - center[:, None]) * spread[:, None]
    gain = jnp.concatenate([norm_gain, their_gain])
    scaled_line = gather_line(low(normed * gain[None, :]))
    above = product(cots[1], out_weight, True, None, jnp.float32)
    below = product(cots[3], out_weight, True, None, jnp.float32)
    their_in = to_sibling(weight_in)
    got, scaled_line, above, below, their_in, cot0 = fence(
        got, scaled_line, above, below, their_in, cots[0]
    )

    up = y_other(low(above + jnp.where(lower_core, wide(got), 0.0)), 1)
    down = y_other(low(below + jnp.where(lower_core, 0.0, wide(got))), -1)
    scaled_blocks = [scaled_line] + [second_other(scaled_line, -step) for step in (1, 2, 3)]
    active_gradient = product(cot0, out_weight, True, None, jnp.float32)
    in_weight = jnp.concatenate([weight_in, their_in], axis=0)
    up, down, active_gradient, in_weight, *scaled_blocks = fence(
        up, down, active_gradient, in_weight, *scaled_blocks
    )

    scaled_all = by_slot(scaled_blocks, y)
    scaled = [scaled_all[slot * line_rows : (slot + 1) * line_rows] for slot in range(SIDE)]
    got = to_ring(product(scaled[2], in_weight, False))
    above = product(scaled[1], in_weight, False, None, jnp.float32)
    below = product(scaled[3], in_weight, False, None, jnp.float32)
    active_gradient = active_gradient + wide(up) + wide(down)
    got, above, below, active_gradient, scaled0 = fence(
        got, above, below, active_gradient, scaled[0]
    )
    up = y_other(low(above + jnp.where(lower_core, wide(got), 0.0)), 1)
    down = y_other(low(below + jnp.where(lower_core, 0.0, wide(got))), -1)
    hidden = product(scaled0, in_weight, False, None, jnp.float32)
    up, down, hidden, active_gradient = fence(up, down, hidden, active_gradient)

    hidden = hidden + wide(up) + wide(down)
    lower = 0.5 + 0.5 * lax.erf(hidden * SQRT_HALF)
    active = low(hidden * lower)
    slope = lower + hidden * (PDF_SCALE * jnp.exp(-0.5 * hidden * hidden))

    gradient0 = low(active_gradient * slope)

    def normed_piece(part, slot):
        part = product(part, in_weight, True)
        return part, second_piece(part, slot)

    def branch_piece(part, slot):
        part = product(part, out_weight, False)
        return part, second_piece(part, slot)

    def line_of(pieces):
        total = 0.0
        for slot, (part, got) in enumerate(pieces):
            total = total + wide(jnp.where(home == slot, part, got))
        return total

    gradient1, gradient3 = y_other(gradient0, -1), y_other(gradient0, 1)
    active1, active3 = y_other(active, -1), y_other(active, 1)
    normed0, branch0 = normed_piece(gradient0, 0), branch_piece(active, 0)
    gradient1, gradient3, *normed0 = fence(gradient1, gradient3, *normed0)
    gradient2 = to_ring_back(jnp.where(lower_core, gradient1, gradient3))
    normed1, normed3 = normed_piece(gradient1, 1), normed_piece(gradient3, 3)
    active1 = after(active1, normed1[0], normed3[0])
    active2 = to_ring_back(jnp.where(lower_core, active1, active3))
    branch1, branch3 = branch_piece(active1, 1), branch_piece(active3, 3)
    normed2 = normed_piece(after(gradient2, branch1[0], branch3[0]), 2)
    branch2 = branch_piece(after(active2, normed2[0], normed1[1], normed3[1]), 2)
    slope_all = jnp.concatenate([gradient0, gradient1, gradient2, gradient3], axis=0)
    active_all = jnp.concatenate([active, active1, active2, active3], axis=0)

    slope_later, active_later, _ = fence(slope_all, active_all, branch2[0])
    in_part = low(dot_tokens(scaled_all[:, width:], slope_later))
    out_part = low(dot_tokens(active_later, cot_all[:, width:]))
    in_part, out_part = to_sibling(in_part), to_sibling(out_part)
    in_gradient = dot_tokens(scaled_all[:, :width], slope_later) + wide(in_part)

    normed_total = line_of([normed0, normed1, normed2, normed3])
    crossed = normed_total * wide(scaled_line)
    sums = jnp.stack([jnp.sum(normed_total * gain[None, :], axis=1), jnp.sum(crossed, axis=1)])
    sums = sums + send(sums, lambda x, y, z, core: (x, y ^ 1, z, core))
    sums = sums + send(sums, lambda x, y, z, core: (x, y ^ 2, z, core))
    gain_part = jnp.sum(crossed, axis=0)
    for bit in (1, 2):
        gain_part = gain_part + send(
            gain_part,
            lambda x, y, z, core: (x, y, z ^ bit, core) if core == 0 else (x ^ bit, y, z, core),
        )
    branch_total = line_of([branch0, branch1, branch2, branch3])
    normed_total, branch_total, sums, gain_part, in_gradient, out_part, active_all = fence(
        normed_total, branch_total, sums, gain_part, in_gradient, out_part, active_all
    )

    normed_sent, branch_sent = low(normed_total), low(branch_total)
    values = jnp.concatenate([sums[0], sums[1]])
    count = values.shape[0]
    gain_high, high = low(gain_part), low(values)
    gain_rest, rest = low(gain_part - wide(gain_high)), low(values - wide(high))
    terms = [gain_high, gain_rest, jnp.pad(jnp.concatenate([high, rest]), (0, 2 * (width - count)))]
    terms = [jnp.broadcast_to(term[None, :], (8, 2 * width)) for term in terms]
    pieces = []
    for step in (1, 2, 3):
        some = slice(step * rows, (step + 1) * rows)
        pieces.append(
            to_first(jnp.concatenate([normed_sent[some], branch_sent[some], *terms], axis=0), step)
        )
    out_gradient = dot_tokens(active_all, cot_all[:, :width]) + wide(out_part)
    normed_gradient, branch, gain_part, sums, out_gradient, *pieces = fence(
        normed_total[:rows], branch_total[:rows], gain_part, sums[:, :rows], out_gradient, *pieces
    )
    normed_gradient = normed_gradient + sum(wide(piece[:rows]) for piece in pieces)
    branch = low(branch + sum(wide(piece[rows : 2 * rows]) for piece in pieces))
    means, crosses = sums[0], sums[1]
    for step, piece in zip((1, 2, 3), pieces, strict=True):
        gain_part = gain_part + wide(piece[2 * rows]) + wide(piece[2 * rows + 8])
        some = wide(piece[2 * rows + 16, : 2 * count])
        some = some[:count] + some[count:]
        means = means + some[step * rows : (step + 1) * rows]
        crosses = crosses + some[(SIDE + step) * rows : (SIDE + step + 1) * rows]
    gain_gradient = (gain_part[:width] + to_sibling(gain_part[width:])) / norm_gain
    scaled_gradient = normed_gradient * gain[None, :]
    input_gradient = low(
        spread[:, None]
        * (scaled_gradient - means[:, None] / D - normed * (crosses[:, None] / D))
    )

    theirs = to_sibling(jnp.concatenate([branch[:, width:], input_gradient[:, width:]], axis=1))
    mine = jnp.concatenate([branch[:, :width], input_gradient[:, :width]], axis=1)
    ends = jnp.where(
        lower_core,
        jnp.concatenate([mine, theirs], axis=0),
        jnp.concatenate([theirs, mine], axis=0),
    )
    return (ends[:, :width], ends[:, width:], in_gradient, out_gradient, gain_gradient)


def solution(mesh):
    in_specs = (P("col", "row"), P("row"), P("row", "col"), P("col", "row"), P("col", "row"))
    out_specs = (P("col", "row"), P("col", "row"), P("row", "col"), P("col", "row"), P("row"))
    return jax.shard_map(
        per_device, mesh=mesh, in_specs=in_specs, out_specs=out_specs, check_vma=False
    )
```

```python
import jax
import jax.numpy as jnp
from jax import lax
from jax.sharding import PartitionSpec as P

D = 6144
SIDE = 4
epsilon = 1e-06
SQRT_HALF = 0.7071067811865476
PDF_SCALE = 0.3989422804014327


def device(x, y, z, core):
    return ((y % SIDE) * 2 + core) * SIDE * SIDE + (z % SIDE) * SIDE + x % SIDE


def table(target):
    pairs = []
    for x in range(SIDE):
        for y in range(SIDE):
            for z in range(SIDE):
                for core in range(2):
                    end = target(x, y, z, core)
                    if end is not None:
                        pairs.append((device(x, y, z, core), device(*end)))
    return pairs


def send(value, target):
    return lax.ppermute(value, ("row", "col"), table(target))


def to_sibling(value):
    return send(value, lambda x, y, z, core: (x, y, z, 1 - core))


def to_ring(value):
    return send(value, lambda x, y, z, core: (x, y + 1 - 2 * core, z, core))


def to_first(value, step):
    return send(
        value,
        lambda x, y, z, core: (x + step, y, z, core) if core == 0 else (x, y, z + step, core),
    )


def second_other(value, step):
    return send(
        value,
        lambda x, y, z, core: (x, y, z + step, core) if core == 0 else (x + step, y, z, core),
    )


def second_piece(value, slot):
    def target(x, y, z, core):
        step = (y + slot) % SIDE
        if step == 0:
            return None
        return (x, y, z + step, core) if core == 0 else (x + step, y, z, core)

    return send(value, target)


def to_ring_back(value):
    return send(value, lambda x, y, z, core: (x, y - 1 + 2 * core, z, core))


def fence(*values):
    return lax.optimization_barrier(values)


def after(value, *done):
    return fence(value, *done)[0]


def low(value):
    return value.astype(jnp.bfloat16)


def wide(value):
    return value.astype(jnp.float32)


def product(left, right, by_rows, more=None, kind=jnp.bfloat16):
    contract = (((1,), (1 if by_rows else 0,)), ((), ()))
    value = lax.dot_general(left, right, contract, preferred_element_type=jnp.float32)
    if more is not None:
        value = value + wide(more)
    return value.astype(kind)


def dot_tokens(left, right):
    return lax.dot_general(left, right, (((0,), (0,)), ((), ())), preferred_element_type=jnp.float32)


def my_half(value, core):
    halves = value.reshape(2, value.shape[0] // 2, value.shape[1])
    mine = lax.dynamic_index_in_dim(halves, core, 0, keepdims=False)
    other = lax.dynamic_index_in_dim(halves, 1 - core, 0, keepdims=False)
    return mine, other


def y_other(value, step):
    return send(value, lambda x, y, z, core: (x, y + step, z, core))


def gather_line(own):
    return jnp.concatenate([own] + [to_first(own, -step) for step in (1, 2, 3)], axis=0)


def by_slot(blocks, y):
    rows, columns = blocks[0].shape
    buffer = jnp.zeros((SIDE * rows, columns), blocks[0].dtype)
    for step, block in enumerate(blocks):
        slot = (step - y) % SIDE
        buffer = lax.dynamic_update_slice(buffer, block, (slot * rows, 0))
    return buffer


def per_device(inputs, norm_gain, weight_in, weight_out, cotangent):
    row = lax.axis_index("row")
    core, y = row % 2, row // 2
    lower_core = core == 0
    home = (SIDE - y) % SIDE
    width = weight_in.shape[0]
    rows = inputs.shape[0] // 2

    mine, other = my_half(jnp.concatenate([inputs, cotangent], axis=1), core)
    theirs = to_sibling(other)
    their_out = to_sibling(weight_out)
    their_gain = to_sibling(norm_gain)
    floats = wide(jnp.concatenate([mine[:, :width], theirs[:, :width]], axis=1))
    own_cot = jnp.concatenate([mine[:, width:], theirs[:, width:]], axis=1)

    sums = jnp.stack([jnp.sum(floats, axis=1), jnp.sum(floats * floats, axis=1)])
    cot_line = gather_line(own_cot)
    sums = sums + send(sums, lambda x, y, z, core: (x, y ^ 1, z, core))
    cot_line, sums, their_gain = fence(cot_line, sums, their_gain)

    cot_blocks = [cot_line] + [second_other(cot_line, -step) for step in (1, 2, 3)]
    swapped = send(sums, lambda x, y, z, core: (x, y ^ 2, z, core))
    out_weight = jnp.concatenate([weight_out, their_out], axis=1)
    *cot_blocks, sums, swapped, out_weight, floats = fence(
        *cot_blocks, sums, swapped, out_weight, floats
    )

    cot_all = by_slot(cot_blocks, y)
    line_rows = cot_line.shape[0]
    cots = [cot_all[slot * line_rows : (slot + 1) * line_rows] for slot in range(SIDE)]
    far = product(cots[2], out_weight, True)
    got = to_ring(far)
    sums = after(sums + swapped, far)
    center = sums[0] / D
    spread = lax.rsqrt(sums[1] / D - center * center + epsilon)
    normed = (floats - center[:, None]) * spread[:, None]
    gain = jnp.concatenate([norm_gain, their_gain])
    scaled_line = gather_line(low(normed * gain[None, :]))
    above = product(cots[1], out_weight, True, None, jnp.float32)
    below = product(cots[3], out_weight, True, None, jnp.float32)
    their_in = to_sibling(weight_in)
    got, scaled_line, above, below, their_in, cot0 = fence(
        got, scaled_line, above, below, their_in, cots[0]
    )

    up = y_other(low(above + jnp.where(lower_core, wide(got), 0.0)), 1)
    down = y_other(low(below + jnp.where(lower_core, 0.0, wide(got))), -1)
    scaled_blocks = [scaled_line] + [second_other(scaled_line, -step) for step in (1, 2, 3)]
    active_gradient = product(cot0, out_weight, True, None, jnp.float32)
    in_weight = jnp.concatenate([weight_in, their_in], axis=0)
    up, down, active_gradient, in_weight, *scaled_blocks = fence(
        up, down, active_gradient, in_weight, *scaled_blocks
    )

    scaled_all = by_slot(scaled_blocks, y)
    scaled = [scaled_all[slot * line_rows : (slot + 1) * line_rows] for slot in range(SIDE)]
    got = to_ring(product(scaled[2], in_weight, False))
    above = product(scaled[1], in_weight, False, None, jnp.float32)
    below = product(scaled[3], in_weight, False, None, jnp.float32)
    active_gradient = active_gradient + wide(up) + wide(down)
    got, above, below, active_gradient, scaled0 = fence(
        got, above, below, active_gradient, scaled[0]
    )
    up = y_other(low(above + jnp.where(lower_core, wide(got), 0.0)), 1)
    down = y_other(low(below + jnp.where(lower_core, 0.0, wide(got))), -1)
    hidden = product(scaled0, in_weight, False, None, jnp.float32)
    up, down, hidden, active_gradient = fence(up, down, hidden, active_gradient)

    hidden = hidden + wide(up) + wide(down)
    lower = 0.5 + 0.5 * lax.erf(hidden * SQRT_HALF)
    active = low(hidden * lower)
    slope = lower + hidden * (PDF_SCALE * jnp.exp(-0.5 * hidden * hidden))

    gradient0 = low(active_gradient * slope)

    def normed_piece(part, slot):
        part = product(part, in_weight, True)
        return part, second_piece(part, slot)

    def branch_piece(part, slot):
        part = product(part, out_weight, False)
        return part, second_piece(part, slot)

    def line_of(pieces):
        total = 0.0
        for slot, (part, got) in enumerate(pieces):
            total = total + wide(jnp.where(home == slot, part, got))
        return total

    gradient1, gradient3 = y_other(gradient0, -1), y_other(gradient0, 1)
    active1, active3 = y_other(active, -1), y_other(active, 1)
    normed0, branch0 = normed_piece(gradient0, 0), branch_piece(active, 0)
    gradient1, gradient3, *normed0 = fence(gradient1, gradient3, *normed0)
    gradient2 = to_ring_back(jnp.where(lower_core, gradient1, gradient3))
    normed1, normed3 = normed_piece(gradient1, 1), normed_piece(gradient3, 3)
    active1 = after(active1, normed1[0], normed3[0])
    active2 = to_ring_back(jnp.where(lower_core, active1, active3))
    branch1, branch3 = branch_piece(active1, 1), branch_piece(active3, 3)
    normed2 = normed_piece(after(gradient2, branch1[0], branch3[0]), 2)
    branch2 = branch_piece(after(active2, normed2[0], normed1[1], normed3[1]), 2)
    slope_all = jnp.concatenate([gradient0, gradient1, gradient2, gradient3], axis=0)
    active_all = jnp.concatenate([active, active1, active2, active3], axis=0)

    slope_later, active_later, _ = fence(slope_all, active_all, branch2[0])
    in_part = low(dot_tokens(scaled_all[:, width:], slope_later))
    out_part = low(dot_tokens(active_later, cot_all[:, width:]))
    in_part, out_part = to_sibling(in_part), to_sibling(out_part)
    in_gradient = dot_tokens(scaled_all[:, :width], slope_later) + wide(in_part)

    normed_total = line_of([normed0, normed1, normed2, normed3])
    crossed = normed_total * wide(scaled_line)
    sums = jnp.stack([jnp.sum(normed_total * gain[None, :], axis=1), jnp.sum(crossed, axis=1)])
    sums = sums + send(sums, lambda x, y, z, core: (x, y ^ 1, z, core))
    sums = sums + send(sums, lambda x, y, z, core: (x, y ^ 2, z, core))
    gain_part = jnp.sum(crossed, axis=0)
    branch_total = line_of([branch0, branch1, branch2, branch3])
    normed_total, branch_total, sums, gain_part, in_gradient, out_part, active_all = fence(
        normed_total, branch_total, sums, gain_part, in_gradient, out_part, active_all
    )

    normed_sent, branch_sent = low(normed_total), low(branch_total)
    values = jnp.concatenate([sums[0], sums[1]])
    count = values.shape[0]
    gain_high, high = low(gain_part), low(values)
    gain_rest, rest = low(gain_part - wide(gain_high)), low(values - wide(high))
    terms = [gain_high, gain_rest, jnp.pad(jnp.concatenate([high, rest]), (0, 2 * (width - count)))]
    terms = [jnp.broadcast_to(term[None, :], (8, 2 * width)) for term in terms]
    pieces = []
    for step in (1, 2, 3):
        some = slice(step * rows, (step + 1) * rows)
        pieces.append(
            to_first(jnp.concatenate([normed_sent[some], branch_sent[some], *terms], axis=0), step)
        )
    out_gradient = dot_tokens(active_all, cot_all[:, :width]) + wide(out_part)
    normed_gradient, branch, gain_part, sums, out_gradient, *pieces = fence(
        normed_total[:rows], branch_total[:rows], gain_part, sums[:, :rows], out_gradient, *pieces
    )
    normed_gradient = normed_gradient + sum(wide(piece[:rows]) for piece in pieces)
    branch = low(branch + sum(wide(piece[rows : 2 * rows]) for piece in pieces))
    means, crosses = sums[0], sums[1]
    for step, piece in zip((1, 2, 3), pieces, strict=True):
        gain_part = gain_part + wide(piece[2 * rows]) + wide(piece[2 * rows + 8])
        some = wide(piece[2 * rows + 16, : 2 * count])
        some = some[:count] + some[count:]
        means = means + some[step * rows : (step + 1) * rows]
        crosses = crosses + some[(SIDE + step) * rows : (SIDE + step + 1) * rows]
    gain_part = gain_part + sum(second_other(gain_part, step) for step in (1, 2, 3))
    gain_gradient = (gain_part[:width] + to_sibling(gain_part[width:])) / norm_gain
    scaled_gradient = normed_gradient * gain[None, :]
    input_gradient = low(
        spread[:, None]
        * (scaled_gradient - means[:, None] / D - normed * (crosses[:, None] / D))
    )

    theirs = to_sibling(jnp.concatenate([branch[:, width:], input_gradient[:, width:]], axis=1))
    mine = jnp.concatenate([branch[:, :width], input_gradient[:, :width]], axis=1)
    ends = jnp.where(
        lower_core,
        jnp.concatenate([mine, theirs], axis=0),
        jnp.concatenate([theirs, mine], axis=0),
    )
    return (ends[:, :width], ends[:, width:], in_gradient, out_gradient, gain_gradient)


def solution(mesh):
    in_specs = (P("col", "row"), P("row"), P("row", "col"), P("col", "row"), P("col", "row"))
    out_specs = (P("col", "row"), P("col", "row"), P("row", "col"), P("col", "row"), P("row"))
    return jax.shard_map(
        per_device, mesh=mesh, in_specs=in_specs, out_specs=out_specs, check_vma=False
    )
```

```python
import jax
import jax.numpy as jnp
from jax import lax
from jax.sharding import PartitionSpec as P

D = 6144
SIDE = 4
epsilon = 1e-06
SQRT_HALF = 0.7071067811865476
PDF_SCALE = 0.3989422804014327


def device(x, y, z, core):
    return ((y % SIDE) * 2 + core) * SIDE * SIDE + (z % SIDE) * SIDE + x % SIDE


def table(target):
    pairs = []
    for x in range(SIDE):
        for y in range(SIDE):
            for z in range(SIDE):
                for core in range(2):
                    end = target(x, y, z, core)
                    if end is not None:
                        pairs.append((device(x, y, z, core), device(*end)))
    return pairs


def send(value, target):
    return lax.ppermute(value, ("row", "col"), table(target))


def to_sibling(value):
    return send(value, lambda x, y, z, core: (x, y, z, 1 - core))


def to_ring(value):
    return send(value, lambda x, y, z, core: (x, y + 1 - 2 * core, z, core))


def to_first(value, step):
    return send(
        value,
        lambda x, y, z, core: (x + step, y, z, core) if core == 0 else (x, y, z + step, core),
    )


def second_other(value, step):
    return send(
        value,
        lambda x, y, z, core: (x, y, z + step, core) if core == 0 else (x + step, y, z, core),
    )


def second_piece(value, slot):
    def target(x, y, z, core):
        step = (y + slot) % SIDE
        if step == 0:
            return None
        return (x, y, z + step, core) if core == 0 else (x + step, y, z, core)

    return send(value, target)


def to_ring_back(value):
    return send(value, lambda x, y, z, core: (x, y - 1 + 2 * core, z, core))


def fence(*values):
    return lax.optimization_barrier(values)


def after(value, *done):
    return fence(value, *done)[0]


def low(value):
    return value.astype(jnp.bfloat16)


def wide(value):
    return value.astype(jnp.float32)


def product(left, right, by_rows, more=None, kind=jnp.bfloat16):
    contract = (((1,), (1 if by_rows else 0,)), ((), ()))
    value = lax.dot_general(left, right, contract, preferred_element_type=jnp.float32)
    if more is not None:
        value = value + wide(more)
    return value.astype(kind)


def dot_tokens(left, right):
    return lax.dot_general(left, right, (((0,), (0,)), ((), ())), preferred_element_type=jnp.float32)


def my_half(value, core):
    halves = value.reshape(2, value.shape[0] // 2, value.shape[1])
    mine = lax.dynamic_index_in_dim(halves, core, 0, keepdims=False)
    other = lax.dynamic_index_in_dim(halves, 1 - core, 0, keepdims=False)
    return mine, other


def y_other(value, step):
    return send(value, lambda x, y, z, core: (x, y + step, z, core))


def gather_line(own):
    return jnp.concatenate([own] + [to_first(own, -step) for step in (1, 2, 3)], axis=0)


def by_slot(blocks, y):
    rows, columns = blocks[0].shape
    buffer = jnp.zeros((SIDE * rows, columns), blocks[0].dtype)
    for step, block in enumerate(blocks):
        slot = (step - y) % SIDE
        buffer = lax.dynamic_update_slice(buffer, block, (slot * rows, 0))
    return buffer


def per_device(inputs, norm_gain, weight_in, weight_out, cotangent):
    row = lax.axis_index("row")
    core, y = row % 2, row // 2
    lower_core = core == 0
    home = (SIDE - y) % SIDE
    width = weight_in.shape[0]
    rows = inputs.shape[0] // 2

    mine, other = my_half(jnp.concatenate([inputs, cotangent], axis=1), core)
    theirs = to_sibling(other)
    their_out = to_sibling(weight_out)
    their_gain = to_sibling(norm_gain)
    floats = wide(jnp.concatenate([mine[:, :width], theirs[:, :width]], axis=1))
    own_cot = jnp.concatenate([mine[:, width:], theirs[:, width:]], axis=1)

    sums = jnp.stack([jnp.sum(floats, axis=1), jnp.sum(floats * floats, axis=1)])
    cot_line = gather_line(own_cot)
    sums = sums + send(sums, lambda x, y, z, core: (x, y ^ 1, z, core))
    cot_line, sums, their_gain = fence(cot_line, sums, their_gain)

    cot_blocks = [cot_line] + [second_other(cot_line, -step) for step in (1, 2, 3)]
    swapped = send(sums, lambda x, y, z, core: (x, y ^ 2, z, core))
    out_weight = jnp.concatenate([weight_out, their_out], axis=1)
    *cot_blocks, sums, swapped, out_weight, floats = fence(
        *cot_blocks, sums, swapped, out_weight, floats
    )

    cot_all = by_slot(cot_blocks, y)
    line_rows = cot_line.shape[0]
    cots = [cot_all[slot * line_rows : (slot + 1) * line_rows] for slot in range(SIDE)]
    far = product(cots[2], out_weight, True)
    got = to_ring(far)
    sums = after(sums + swapped, far)
    center = sums[0] / D
    spread = lax.rsqrt(sums[1] / D - center * center + epsilon)
    normed = (floats - center[:, None]) * spread[:, None]
    gain = jnp.concatenate([norm_gain, their_gain])
    scaled_line = gather_line(low(normed * gain[None, :]))
    above = product(cots[1], out_weight, True, None, jnp.float32)
    below = product(cots[3], out_weight, True, None, jnp.float32)
    their_in = to_sibling(weight_in)
    got, scaled_line, above, below, their_in, cot0 = fence(
        got, scaled_line, above, below, their_in, cots[0]
    )

    up = y_other(low(above + jnp.where(lower_core, wide(got), 0.0)), 1)
    down = y_other(low(below + jnp.where(lower_core, 0.0, wide(got))), -1)
    scaled_blocks = [scaled_line] + [second_other(scaled_line, -step) for step in (1, 2, 3)]
    active_gradient = product(cot0, out_weight, True, None, jnp.float32)
    in_weight = jnp.concatenate([weight_in, their_in], axis=0)
    up, down, active_gradient, in_weight, *scaled_blocks = fence(
        up, down, active_gradient, in_weight, *scaled_blocks
    )

    scaled_all = by_slot(scaled_blocks, y)
    scaled = [scaled_all[slot * line_rows : (slot + 1) * line_rows] for slot in range(SIDE)]
    got = to_ring(product(scaled[2], in_weight, False))
    above = product(scaled[1], in_weight, False, None, jnp.float32)
    below = product(scaled[3], in_weight, False, None, jnp.float32)
    active_gradient = active_gradient + wide(up) + wide(down)
    got, above, below, active_gradient, scaled0 = fence(
        got, above, below, active_gradient, scaled[0]
    )
    up = y_other(low(above + jnp.where(lower_core, wide(got), 0.0)), 1)
    down = y_other(low(below + jnp.where(lower_core, 0.0, wide(got))), -1)
    hidden = product(scaled0, in_weight, False, None, jnp.float32)
    up, down, hidden, active_gradient = fence(up, down, hidden, active_gradient)

    hidden = hidden + wide(up) + wide(down)
    lower = 0.5 + 0.5 * lax.erf(hidden * SQRT_HALF)
    active = low(hidden * lower)
    slope = lower + hidden * (PDF_SCALE * jnp.exp(-0.5 * hidden * hidden))

    gradient0 = low(active_gradient * slope)

    def normed_piece(part, slot):
        part = product(part, in_weight, True)
        return part, second_piece(part, slot)

    def branch_piece(part, slot):
        part = product(part, out_weight, False)
        return part, second_piece(part, slot)

    def line_of(pieces):
        total = 0.0
        for slot, (part, got) in enumerate(pieces):
            total = total + wide(jnp.where(home == slot, part, got))
        return total

    gradient1, gradient3 = y_other(gradient0, -1), y_other(gradient0, 1)
    active1, active3 = y_other(active, -1), y_other(active, 1)
    normed0, branch0 = normed_piece(gradient0, 0), branch_piece(active, 0)
    gradient1, gradient3, *normed0 = fence(gradient1, gradient3, *normed0)
    gradient2 = to_ring_back(jnp.where(lower_core, gradient1, gradient3))
    normed1, normed3 = normed_piece(gradient1, 1), normed_piece(gradient3, 3)
    active1 = after(active1, normed1[0], normed3[0])
    active2 = to_ring_back(jnp.where(lower_core, active1, active3))
    branch1, branch3 = branch_piece(active1, 1), branch_piece(active3, 3)
    normed2 = normed_piece(after(gradient2, branch1[0], branch3[0]), 2)
    branch2 = branch_piece(after(active2, normed2[0], normed1[1], normed3[1]), 2)
    slope_all = jnp.concatenate([gradient0, gradient1, gradient2, gradient3], axis=0)
    active_all = jnp.concatenate([active, active1, active2, active3], axis=0)

    slope_later, active_later, _ = fence(slope_all, active_all, branch2[0])
    in_part = low(dot_tokens(scaled_all[:, width:], slope_later))
    out_part = low(dot_tokens(active_later, cot_all[:, width:]))
    in_part, out_part = to_sibling(in_part), to_sibling(out_part)
    in_gradient = dot_tokens(scaled_all[:, :width], slope_later) + wide(in_part)

    normed_total = line_of([normed0, normed1, normed2, normed3])
    crossed = normed_total * wide(scaled_line)
    sums = jnp.stack([jnp.sum(normed_total * gain[None, :], axis=1), jnp.sum(crossed, axis=1)])
    sums = sums + sum(y_other(sums, step) for step in (1, 2, 3))
    gain_part = jnp.sum(crossed, axis=0)
    gain_part = gain_part[:width] + to_sibling(gain_part[width:])
    branch_total = line_of([branch0, branch1, branch2, branch3])
    normed_total, branch_total, sums, gain_part, in_gradient, out_part, active_all = fence(
        normed_total, branch_total, sums, gain_part, in_gradient, out_part, active_all
    )

    normed_sent, branch_sent = low(normed_total), low(branch_total)
    values = jnp.concatenate([sums[0], sums[1]])
    count = values.shape[0]
    gain_high, high = low(gain_part), low(values)
    gain_rest, rest = low(gain_part - wide(gain_high)), low(values - wide(high))
    terms = [
        jnp.concatenate([gain_high, gain_rest]),
        jnp.pad(jnp.concatenate([high, rest]), (0, 2 * (width - count))),
    ]
    terms = [jnp.broadcast_to(term[None, :], (8, 2 * width)) for term in terms]
    pieces = []
    for step in (1, 2, 3):
        some = slice(step * rows, (step + 1) * rows)
        pieces.append(
            to_first(jnp.concatenate([normed_sent[some], branch_sent[some], *terms], axis=0), step)
        )
    out_gradient = dot_tokens(active_all, cot_all[:, :width]) + wide(out_part)
    normed_gradient, branch, gain_part, sums, out_gradient, *pieces = fence(
        normed_total[:rows], branch_total[:rows], gain_part, sums[:, :rows], out_gradient, *pieces
    )
    normed_gradient = normed_gradient + sum(wide(piece[:rows]) for piece in pieces)
    branch = low(branch + sum(wide(piece[rows : 2 * rows]) for piece in pieces))
    means, crosses = sums[0], sums[1]
    for step, piece in zip((1, 2, 3), pieces, strict=True):
        gain_part = gain_part + wide(piece[2 * rows, :width]) + wide(piece[2 * rows, width:])
        some = wide(piece[2 * rows + 8, : 2 * count])
        some = some[:count] + some[count:]
        means = means + some[step * rows : (step + 1) * rows]
        crosses = crosses + some[(SIDE + step) * rows : (SIDE + step + 1) * rows]
    gain_part = gain_part + sum(second_other(gain_part, step) for step in (1, 2, 3))
    gain_gradient = gain_part / norm_gain
    scaled_gradient = normed_gradient * gain[None, :]
    input_gradient = low(
        spread[:, None]
        * (scaled_gradient - means[:, None] / D - normed * (crosses[:, None] / D))
    )

    theirs = to_sibling(jnp.concatenate([branch[:, width:], input_gradient[:, width:]], axis=1))
    mine = jnp.concatenate([branch[:, :width], input_gradient[:, :width]], axis=1)
    ends = jnp.where(
        lower_core,
        jnp.concatenate([mine, theirs], axis=0),
        jnp.concatenate([theirs, mine], axis=0),
    )
    return (ends[:, :width], ends[:, width:], in_gradient, out_gradient, gain_gradient)


def solution(mesh):
    in_specs = (P("col", "row"), P("row"), P("row", "col"), P("col", "row"), P("col", "row"))
    out_specs = (P("col", "row"), P("col", "row"), P("row", "col"), P("col", "row"), P("row"))
    return jax.shard_map(
        per_device, mesh=mesh, in_specs=in_specs, out_specs=out_specs, check_vma=False
    )
```
